512 devices in a mesh: row: 32 (over y, z_hi, core), col: 16 (over x, z_lo).
Axes of the slice: x: 4, y: 4, z: 16 (z_hi: 4, z_lo: 4; z = z_hi * 4 + z_lo), core: 2. Of those that a mesh axis runs over, the one named last changes fastest.
Arguments:
- features: bfloat16 [65536, 256], P(('col', 'row')), may hold values from -6 to 6
- grad_out: bfloat16 [65536, 256], P(('row', 'col')), may hold values from -6 to 6
- weight: bfloat16 [256, 256], replicated, may hold values from -0.375 to 0.375
- tiles: bfloat16 [32, 16, 96, 128, 128], P('row', 'col')
- coords: int32 [32, 16, 96, 2], P('row', 'col'), may hold values from 0 to 31, as said below
Outputs:
- grad_features: bfloat16 [65536, 256], P(('col', 'row'))
- grad_weight: float32 [256, 256], replicated
The draws below stay inside these ranges and needn't reach their ends.
Inputs may be any that keep to these rules, and one draw needn't show every extreme that they name: `coords`: the 96 (tile row, tile column) pairs of one device are distinct; tile rows lie below 16, tile columns below 32.
All inputs are finite; a program needn't handle non-finite values.
Results may differ from the reference program's by a relative error of at most 0.029.
Values may be sent and summed in bfloat16 or wider, within the bound.
No kernel may reach another device: no remote copies, remote signals or barrier semaphores. Data moves between devices by JAX's collectives and lax.ppermute only.
A program may use at most 64 MiB of HBM per device.

```python
import math
import jax
import jax.numpy as jnp
from jax import lax

H = 256
TILE = 128
ND = 128
NODES = 65536
N_ROW = 32
N_COL = 16


def draw_tiles(key, part):
    key = jax.random.fold_in(key, 11)
    key_mask, key_rate, key_value, key_live, key_full = jax.random.split(key, 5)
    row_tiles = ND * N_COL // TILE
    col_tiles = ND * N_ROW // TILE
    slots = max(1, row_tiles * col_tiles * 3 // 16)
    shape = (N_ROW, N_COL, slots, TILE, TILE)
    rate = jax.random.randint(key_rate, (N_ROW, N_COL, slots, 1, 1), 1, 6)
    edges = jax.random.randint(key_mask, shape, 0, 32) < rate
    values = jnp.exp(0.5 * jax.random.normal(key_value, shape, jnp.float32))
    live = jax.random.randint(key_live, (N_ROW * N_COL,), max(1, slots // 4), slots + 1)
    fullest = jax.random.randint(key_full, (), 0, N_ROW * N_COL)
    live = jnp.where(jnp.arange(N_ROW * N_COL) == fullest, slots, live).reshape(N_ROW, N_COL, 1)
    alive = (jnp.arange(slots)[None, None, :] < live)[..., None, None]
    scale = 1.0 / math.sqrt(max(1.0, 0.01 * col_tiles * TILE * N_COL))
    return (jnp.where(edges & alive, values, 0.0) * scale).astype(jnp.bfloat16)


def draw_coords(key, part):
    key = jax.random.fold_in(key, 23)
    row_tiles = ND * N_COL // TILE
    col_tiles = ND * N_ROW // TILE
    slots = max(1, row_tiles * col_tiles * 3 // 16)
    keys = jax.random.split(key, N_ROW * N_COL)
    picks = jax.vmap(lambda one: jax.random.permutation(one, row_tiles * col_tiles)[:slots])(keys)
    picks = picks.astype(jnp.int32)
    pairs = jnp.stack([picks // col_tiles, picks % col_tiles], axis=-1)
    return pairs.reshape(N_ROW, N_COL, slots, 2).astype(jnp.int32)


def levels(stream_key, extent, shards, low, largest):
    loudness = 1.0
    for axis_at, blocks in shards:
        steps = jax.random.uniform(jax.random.fold_in(jax.random.fold_in(stream_key, 6), axis_at), (blocks,), jnp.float32, low / len(shards), largest / len(shards))
        loudness = loudness * jnp.repeat(jnp.exp(steps), extent[axis_at] // blocks).reshape((-1,) + (1,) * (len(extent) - 1 - axis_at))
    return loudness


def bell_draw(rng, extent, scale, bound, cuts=(), held_as=jnp.bfloat16):
    entries = jax.random.normal(rng, extent, jnp.float32) * scale
    if len(cuts) > 0:
        entries = levels(rng, extent, cuts, -0.22, 0.18) * entries
    return jnp.clip(entries, min=-bound, max=bound).astype(held_as)


def setup_inputs(seed: int = 0) -> dict:
    key_of = jax.random.split(jax.random.key(seed), 6)
    features = bell_draw(key_of[0], (NODES, H), 1.0, 6.0, ((0, 512),))
    grad_out = bell_draw(key_of[1], (NODES, H), 1.0, 6.0, ((0, 512),))
    weight = bell_draw(key_of[2], (H, H), H ** -0.5, 0.375)
    tiles = draw_tiles(jax.random.fold_in(key_of[5], 71), 0)
    coords = draw_coords(jax.random.fold_in(key_of[5], 71), 0)
    return {"features": features, "grad_out": grad_out, "weight": weight, "tiles": tiles, "coords": coords}


def silu_slope(value):
    sig = jax.nn.sigmoid(value)
    return sig * (1.0 + value * (1.0 - sig))

def block_term(tile_set, coord_set, source, n_dst, backward):
    width = source.shape[1]
    blocks = source.reshape(-1, TILE, width)
    if backward:
        src_index = coord_set[:, 0]
        dst_index = coord_set[:, 1]
        form = 'kji,kjh->kih'
    else:
        src_index = coord_set[:, 1]
        dst_index = coord_set[:, 0]
        form = 'kij,kjh->kih'
    picked = jnp.take(blocks, src_index, axis=0).astype(jnp.float32)
    product = jnp.einsum(form, tile_set.astype(jnp.float32), picked, precision=lax.Precision.HIGHEST)
    summed = jnp.zeros((n_dst, TILE, width), jnp.float32).at[dst_index].add(product)
    return summed.reshape(-1, width).astype(jnp.bfloat16)

def reference(features, grad_out, weight, tiles, coords):
    nodes = features.shape[0]
    width = features.shape[1]
    row_len = nodes // N_ROW
    col_len = nodes // N_COL
    row_tiles = row_len // TILE
    col_tiles = col_len // TILE

    def forward_row(rindex):

        def step(total, cindex):
            source = lax.dynamic_slice_in_dim(features, cindex * col_len, col_len, 0)
            term = block_term(tiles[rindex, cindex], coords[rindex, cindex], source, row_tiles, False)
            return (total + term.astype(jnp.float32), None)
        total, _ = lax.scan(step, jnp.zeros((row_len, width), jnp.float32), jnp.arange(N_COL, dtype=jnp.int32))
        return total.astype(jnp.bfloat16)
    aggregated = lax.map(forward_row, jnp.arange(N_ROW, dtype=jnp.int32)).reshape(nodes, width)
    pre = jnp.dot(aggregated, weight, preferred_element_type=jnp.float32)
    slope_grad = (grad_out.astype(jnp.float32) * silu_slope(pre)).astype(jnp.bfloat16)
    grad_weight = jnp.einsum('nh,ng->hg', aggregated.astype(jnp.float32), slope_grad.astype(jnp.float32), precision=lax.Precision.HIGHEST) * (1.0 / math.sqrt(nodes))
    node_grad = jnp.dot(slope_grad, weight.T, preferred_element_type=jnp.float32).astype(jnp.bfloat16)

    def backward_col(cindex):

        def step(total, rindex):
            source = lax.dynamic_slice_in_dim(node_grad, rindex * row_len, row_len, 0)
            term = block_term(tiles[rindex, cindex], coords[rindex, cindex], source, col_tiles, True)
            return (total + term.astype(jnp.float32), None)
        total, _ = lax.scan(step, jnp.zeros((col_len, width), jnp.float32), jnp.arange(N_ROW, dtype=jnp.int32))
        return total.astype(jnp.bfloat16)
    grad_features = lax.map(backward_col, jnp.arange(N_COL, dtype=jnp.int32)).reshape(nodes, width)
    return (grad_features, grad_weight)
```

```python
import functools
import math

import jax
import jax.numpy as jnp
from jax import lax
from jax.experimental import pallas as pl
from jax.experimental.pallas import tpu as pltpu
from jax.sharding import Mesh
from jax.sharding import PartitionSpec as P

F32 = jnp.float32
BF16 = jnp.bfloat16
SIZES = {"y": 4, "zh": 4, "co": 2, "x": 4, "zl": 4}
NY, NZH, NCO, NX, NZL = (SIZES[a] for a in ("y", "zh", "co", "x", "zl"))
ROW = ("y", "zh", "co")
COL = ("x", "zl")
T = 128
H = 256
GROUP = 8
VMEM_LIMIT = 40 * 1024 * 1024


def exchange(value, axis):
    return lax.all_to_all(value, axis, 0, 0, tiled=True)


def spread(value, axis):
    return exchange(jnp.broadcast_to(value[None], (SIZES[axis],) + value.shape), axis)


def swap_cores(value):
    return lax.ppermute(value, "co", [(0, 1), (1, 0)])


def split_pair(value):
    high = value.astype(BF16)
    low = (value - high.astype(F32)).astype(BF16)
    return jnp.concatenate([high[:, :T], high[:, T:], low[:, :T], low[:, T:]], axis=0)


def join_pair(rows):
    n = rows.shape[0] // 4
    rows = rows.astype(F32)
    high = jnp.concatenate([rows[:n], rows[n : 2 * n]], axis=1)
    low = jnp.concatenate([rows[2 * n : 3 * n], rows[3 * n :]], axis=1)
    return high + low


def forward_kernel(coords, core, tiles_hbm, own_hbm, other_hbm, out, tiles, source, total, sem, sem_x):
    slots = tiles.shape[0]
    half = own_hbm.shape[0]
    groups = slots // GROUP

    def tile_copy(g):
        at = pl.ds(g * GROUP, GROUP)
        return pltpu.make_async_copy(tiles_hbm.at[at], tiles.at[at], sem.at[g])

    copies = [
        pltpu.make_async_copy(own_hbm, source.at[pl.ds(0, half)], sem_x.at[0]),
        pltpu.make_async_copy(other_hbm, source.at[pl.ds(half, half)], sem_x.at[1]),
    ]
    for c in copies:
        c.start()
    for g in range(groups):
        tile_copy(g).start()
    total[...] = jnp.zeros_like(total)
    me = core[0]
    for c in copies:
        c.wait()

    def step(g, carry):
        tile_copy(g).wait()
        products = []
        for u in range(GROUP):
            k = g * GROUP + u
            j = coords[2 * k + 1]
            at = ((j & 1) ^ me) * half + (j >> 1)
            products.append(jnp.dot(tiles[k], source[at], preferred_element_type=F32))
        for u in range(GROUP):
            i = coords[2 * (g * GROUP + u)]
            total[i] += products[u]
        return carry

    lax.fori_loop(0, groups, step, 0)
    out[...] = total[...].astype(out.dtype)


def dense_kernel(parts, weight, grad_out, out):
    total = parts[0].astype(F32)
    for s in range(1, parts.shape[0]):
        total = total + parts[s].astype(F32)
    aggregated = total.astype(BF16)
    pre = jnp.dot(aggregated, weight[...], preferred_element_type=F32)
    sig = jax.nn.sigmoid(pre)
    slope = grad_out[...].astype(F32) * (sig * (1.0 + pre * (1.0 - sig)))
    slope_t = slope.T.astype(BF16)
    agg_t = aggregated.astype(F32).T.astype(BF16)
    share = H // (NX * NZL)
    for l in range(NZL):
        out[l, :H] = slope_t
        for x in range(NX):
            at = (x * NZL + l) * share
            out[l, H + x * share : H + (x + 1) * share] = agg_t[at : at + share]


def backward_kernel(coords, core, tiles_hbm, grads, weight, mine, other, tiles, source, total, sem):
    slots = tiles.shape[0]
    blocks = grads.shape[0]
    half = total.shape[0] // 2
    groups = slots // GROUP

    def tile_copy(g):
        at = pl.ds(g * GROUP, GROUP)
        return pltpu.make_async_copy(tiles_hbm.at[at], tiles.at[at], sem.at[g])

    for g in range(groups):
        tile_copy(g).start()
    total[...] = jnp.zeros_like(total)
    me = core[0]
    share = grads.shape[1] - H
    weight_grad = jnp.zeros((share, H), F32)
    for c in range(blocks):
        slope_t = grads[c, :H]
        source[c] = jnp.dot(weight[...], slope_t, preferred_element_type=F32).astype(BF16)
        weight_grad = weight_grad + lax.dot_general(
            grads[c, H:], slope_t, (((1,), (1,)), ((), ())), preferred_element_type=F32
        )

    def step(g, carry):
        tile_copy(g).wait()
        products = []
        for u in range(GROUP):
            k = g * GROUP + u
            products.append(jnp.dot(source[coords[2 * k]], tiles[k], preferred_element_type=F32))
        for u in range(GROUP):
            j = coords[2 * (g * GROUP + u) + 1]
            at = ((j & 1) ^ me) * half + (j >> 1)
            total[at] += products[u]
        return carry

    lax.fori_loop(0, groups, step, 0)
    pair = split_pair(weight_grad)
    for value, first in ((mine, 0), (other, half)):
        for p in range(half):
            value[p * H : (p + 1) * H] = total[first + p].astype(BF16)
        value[half * H :] = pair


def core_sum_kernel(mine, other, out):
    rows = (mine.shape[0] - out.shape[1]) // (NY - 1)
    pair = split_pair(join_pair(mine[NY * rows :]) + join_pair(other[NY * rows :]))
    for y in range(NY):
        at = pl.ds(y * rows, rows)
        out[y, :rows] = (mine[at].astype(F32) + other[at].astype(F32)).astype(BF16)
        out[y, rows:] = pair


def y_sum_kernel(parts, out):
    rows = NZH * H
    pair = join_pair(parts[0, rows:])
    for s in range(1, NY):
        pair = pair + join_pair(parts[s, rows:])
    pair = split_pair(pair)
    for z in range(NZH):
        at = pl.ds(z * H, H)
        total = parts[0, at].astype(F32)
        for s in range(1, NY):
            total = total + parts[s, at].astype(F32)
        out[z, :H] = total.astype(BF16)
        out[z, H:] = pair


def last_sum_kernel(parts, out, weight_grad):
    total = parts[0, :H].astype(F32)
    pair = join_pair(parts[0, H:])
    for s in range(1, NZH):
        total = total + parts[s, :H].astype(F32)
        pair = pair + join_pair(parts[s, H:])
    out[...] = total.T.astype(BF16)
    weight_grad[...] = pair


def shape(*dims, dtype=BF16):
    return jax.ShapeDtypeStruct(dims, dtype)


def call(body, outs, ins, flops=0, scratch=(), name=None):
    moved = sum(math.prod(o.shape) * o.dtype.itemsize for o in outs)
    single = len(outs) == 1
    vmem = pl.BlockSpec(memory_space=pltpu.VMEM)
    return pl.pallas_call(
        body,
        out_shape=outs[0] if single else tuple(outs),
        in_specs=[pl.BlockSpec(memory_space=s) for s in ins],
        out_specs=vmem if single else tuple(vmem for _ in outs),
        scratch_shapes=list(scratch),
        compiler_params=pltpu.CompilerParams(vmem_limit_bytes=VMEM_LIMIT),
        cost_estimate=pl.CostEstimate(flops=flops, bytes_accessed=4 * moved, transcendentals=0),
        name=name,
    )


def on_device(features, grad_out, weight, tiles, coords):
    tile_set = tiles[0, 0]
    coord_set = coords[0, 0].reshape(-1)
    slots = tile_set.shape[0]
    groups = slots // GROUP
    core = lax.axis_index("co").astype(jnp.int32).reshape(1)
    nodes = T * math.prod(SIZES.values())
    row_tiles, col_tiles = NX * NZL, NY * NZH * NCO
    half = col_tiles // 2
    share = H // row_tiles
    pair_rows = 4 * share
    SMEM, VMEM, ANY = pltpu.SMEM, pltpu.VMEM, pl.ANY
    product_flops = 2 * slots * T * T * H

    with jax.named_scope("gather_features"):
        own = spread(spread(features, "zh").reshape(NZH, T, H), "y").reshape(half, T, H)
        other = swap_cores(own)
    part = call(
        forward_kernel,
        [shape(row_tiles, T, H)],
        [SMEM, SMEM, ANY, ANY, ANY],
        flops=product_flops,
        scratch=[
            VMEM((slots, T, T), BF16),
            VMEM((col_tiles, T, H), BF16),
            VMEM((row_tiles, T, H), F32),
            pltpu.SemaphoreType.DMA((groups,)),
            pltpu.SemaphoreType.DMA((2,)),
        ],
        name="forward_products",
    )(coord_set, core, tile_set, own, other)
    with jax.named_scope("sum_over_col"):
        part = exchange(part.reshape(NX, NZL, T, H), "x")
        part = jnp.sum(part.astype(F32), axis=0).astype(BF16)
        part = exchange(part, "zl")
    grads = call(
        dense_kernel,
        [shape(NZL, H + NX * share, T)],
        [VMEM] * 3,
        flops=2 * T * H * H,
        name="dense",
    )(part, weight, grad_out)
    with jax.named_scope("gather_gradients"):
        grads = exchange(grads, "zl")
        common = jnp.broadcast_to(grads[None, :, :H], (NX, NZL, H, T))
        slices = grads[:, H:].reshape(NZL, NX, share, T).transpose(1, 0, 2, 3)
        grads = exchange(jnp.concatenate([common, slices], axis=2), "x")
        grads = grads.reshape(row_tiles, H + share, T)
    mine, theirs = call(
        backward_kernel,
        [shape(half * H + pair_rows, T), shape(half * H + pair_rows, T)],
        [SMEM, SMEM, ANY, VMEM, VMEM],
        flops=product_flops,
        scratch=[
            VMEM((slots, T, T), BF16),
            VMEM((row_tiles, H, T), BF16),
            VMEM((col_tiles, H, T), F32),
            pltpu.SemaphoreType.DMA((groups,)),
        ],
        name="backward_products",
    )(coord_set, core, tile_set, grads, weight)
    with jax.named_scope("sum_over_row"):
        theirs = swap_cores(theirs)
        back = call(core_sum_kernel, [shape(NY, NZH * H + pair_rows, T)], [VMEM] * 2, name="core_sum")(
            mine, theirs
        )
        back = exchange(back, "y")
        back = call(y_sum_kernel, [shape(NZH, H + pair_rows, T)], [VMEM], name="y_sum")(back)
        back = exchange(back, "zh")
        grad_features, weight_grad = call(
            last_sum_kernel, [shape(T, H), shape(share, H, dtype=F32)], [VMEM], name="last_sum"
        )(back)
    with jax.named_scope("gather_weight_grad"):
        weight_grad = spread(weight_grad, "zl").reshape(NZL * share, H)
        weight_grad = spread(weight_grad, "x").reshape(H, H)
    return grad_features, weight_grad * (1.0 / math.sqrt(nodes))


def solution(mesh):
    fine = Mesh(mesh.devices.reshape(tuple(SIZES.values())), tuple(SIZES))
    in_specs = (
        P(COL + ROW, None),
        P(ROW + COL, None),
        P(),
        P(ROW, COL, None, None, None),
        P(ROW, COL, None, None),
    )
    out_specs = (P(COL + ROW, None), P())
    return jax.shard_map(
        on_device, mesh=fine, in_specs=in_specs, out_specs=out_specs, check_vma=False
    )
```

```python
import math

import jax
import jax.numpy as jnp
from jax import lax
from jax.experimental import pallas as pl
from jax.experimental.pallas import tpu as pltpu
from jax.sharding import Mesh
from jax.sharding import PartitionSpec as P

F32 = jnp.float32
BF16 = jnp.bfloat16
SIZES = {"y": 4, "zh": 4, "co": 2, "x": 4, "zl": 4}
NY, NZH, NCO, NX, NZL = (SIZES[a] for a in ("y", "zh", "co", "x", "zl"))
ROW = ("y", "zh", "co")
COL = ("x", "zl")
T = 128
H = 256
GROUP = 32
VMEM_LIMIT = 40 * 1024 * 1024


def exchange(value, axis):
    return lax.all_to_all(value, axis, 0, 0, tiled=True)


def spread(value, axis):
    return exchange(jnp.broadcast_to(value[None], (SIZES[axis],) + value.shape), axis)


def swap_cores(value):
    return lax.ppermute(value, "co", [(0, 1), (1, 0)])


def split_pair(value):
    high = value.astype(BF16)
    low = (value - high.astype(F32)).astype(BF16)
    return jnp.concatenate([high[:, :T], high[:, T:], low[:, :T], low[:, T:]], axis=0)


def join_pair(rows):
    n = rows.shape[0] // 4
    rows = rows.astype(F32)
    high = jnp.concatenate([rows[:n], rows[n : 2 * n]], axis=1)
    low = jnp.concatenate([rows[2 * n : 3 * n], rows[3 * n :]], axis=1)
    return high + low


def forward_kernel(coords, core, tiles, own, other, out, source, total):
    half = own.shape[0]
    source[:half] = own[...]
    source[half:] = other[...]
    total[...] = jnp.zeros_like(total)
    me = core[0]

    def step(g, carry):
        products = []
        for u in range(GROUP):
            k = g * GROUP + u
            j = coords[2 * k + 1]
            at = ((j & 1) ^ me) * half + (j >> 1)
            products.append(jnp.dot(tiles[k], source[at], preferred_element_type=F32))
        for u in range(GROUP):
            i = coords[2 * (g * GROUP + u)]
            total[i] += products[u]
        return carry

    lax.fori_loop(0, tiles.shape[0] // GROUP, step, 0)
    out[...] = total[...].astype(out.dtype)


def x_sum_kernel(parts, out):
    total = parts[0].astype(F32)
    for s in range(1, parts.shape[0]):
        total = total + parts[s].astype(F32)
    out[...] = total.astype(BF16)


def dense_kernel(parts, weight, grad_out, out):
    total = parts[0].astype(F32)
    for s in range(1, parts.shape[0]):
        total = total + parts[s].astype(F32)
    aggregated = total.astype(BF16)
    pre = jnp.dot(aggregated, weight[...], preferred_element_type=F32)
    sig = jax.nn.sigmoid(pre)
    slope = grad_out[...].astype(F32) * (sig * (1.0 + pre * (1.0 - sig)))
    slope_t = slope.T.astype(BF16)
    agg_t = aggregated.astype(F32).T.astype(BF16)
    share = H // (NX * NZL)
    for l in range(NZL):
        out[l, :H] = slope_t
        for x in range(NX):
            at = (x * NZL + l) * share
            out[l, H + x * share : H + (x + 1) * share] = agg_t[at : at + share]


def backward_kernel(coords, core, tiles, grads, weight, mine, other, source, total):
    blocks = grads.shape[0]
    half = total.shape[0] // 2
    total[...] = jnp.zeros_like(total)
    me = core[0]
    share = grads.shape[1] - H
    weight_grad = jnp.zeros((share, H), F32)
    for c in range(blocks):
        slope_t = grads[c, :H]
        source[c] = jnp.dot(weight[...], slope_t, preferred_element_type=F32).astype(BF16)
        weight_grad = weight_grad + lax.dot_general(
            grads[c, H:], slope_t, (((1,), (1,)), ((), ())), preferred_element_type=F32
        )

    def step(g, carry):
        products = []
        for u in range(GROUP):
            k = g * GROUP + u
            products.append(jnp.dot(source[coords[2 * k]], tiles[k], preferred_element_type=F32))
        for u in range(GROUP):
            j = coords[2 * (g * GROUP + u) + 1]
            at = ((j & 1) ^ me) * half + (j >> 1)
            total[at] += products[u]
        return carry

    lax.fori_loop(0, tiles.shape[0] // GROUP, step, 0)
    pair = split_pair(weight_grad)
    for value, first in ((mine, 0), (other, half)):
        for p in range(half):
            value[p * H : (p + 1) * H] = total[first + p].astype(BF16)
        value[half * H :] = pair


def core_sum_kernel(mine, other, out):
    rows = (mine.shape[0] - out.shape[1]) // (NY - 1)
    pair = split_pair(join_pair(mine[NY * rows :]) + join_pair(other[NY * rows :]))
    for y in range(NY):
        at = pl.ds(y * rows, rows)
        out[y, :rows] = (mine[at].astype(F32) + other[at].astype(F32)).astype(BF16)
        out[y, rows:] = pair


def y_sum_kernel(parts, out):
    rows = NZH * H
    pair = join_pair(parts[0, rows:])
    for s in range(1, NY):
        pair = pair + join_pair(parts[s, rows:])
    pair = split_pair(pair)
    for z in range(NZH):
        at = pl.ds(z * H, H)
        total = parts[0, at].astype(F32)
        for s in range(1, NY):
            total = total + parts[s, at].astype(F32)
        out[z, :H] = total.astype(BF16)
        out[z, H:] = pair


def last_sum_kernel(parts, out, weight_grad):
    total = parts[0, :H].astype(F32)
    pair = join_pair(parts[0, H:])
    for s in range(1, NZH):
        total = total + parts[s, :H].astype(F32)
        pair = pair + join_pair(parts[s, H:])
    out[...] = total.T.astype(BF16)
    scale = 1.0 / math.sqrt(T * math.prod(SIZES.values()))
    for c in range(NX * NZL):
        weight_grad[c] = pair * scale


def shape(*dims, dtype=BF16):
    return jax.ShapeDtypeStruct(dims, dtype)


def call(body, outs, ins, flops=0, scratch=(), name=None):
    moved = sum(math.prod(o.shape) * o.dtype.itemsize for o in outs)
    single = len(outs) == 1
    vmem = pl.BlockSpec(memory_space=pltpu.VMEM)
    return pl.pallas_call(
        body,
        out_shape=outs[0] if single else tuple(outs),
        in_specs=[pl.BlockSpec(memory_space=s) for s in ins],
        out_specs=vmem if single else tuple(vmem for _ in outs),
        scratch_shapes=list(scratch),
        compiler_params=pltpu.CompilerParams(vmem_limit_bytes=VMEM_LIMIT),
        cost_estimate=pl.CostEstimate(flops=flops, bytes_accessed=4 * moved, transcendentals=0),
        name=name,
    )


def on_device(features, grad_out, weight, tiles, coords):
    tile_set = tiles[0, 0]
    coord_set = coords[0, 0].reshape(-1)
    slots = tile_set.shape[0]
    core = lax.axis_index("co").astype(jnp.int32).reshape(1)
    row_tiles, col_tiles = NX * NZL, NY * NZH * NCO
    half = col_tiles // 2
    share = H // row_tiles
    pair_rows = 4 * share
    SMEM, VMEM = pltpu.SMEM, pltpu.VMEM
    product_flops = 2 * slots * T * T * H

    with jax.named_scope("gather_features"):
        own = spread(spread(features, "zh").reshape(NZH, T, H), "y").reshape(half, T, H)
        other = swap_cores(own)
    part = call(
        forward_kernel,
        [shape(row_tiles, T, H)],
        [SMEM, SMEM, VMEM, VMEM, VMEM],
        flops=product_flops,
        scratch=[VMEM((col_tiles, T, H), BF16), VMEM((row_tiles, T, H), F32)],
        name="forward_products",
    )(coord_set, core, tile_set, own, other)
    with jax.named_scope("sum_over_col"):
        part = exchange(part.reshape(NX, NZL, T, H), "x")
        part = call(x_sum_kernel, [shape(NZL, T, H)], [VMEM], name="x_sum")(part)
        part = exchange(part, "zl")
    grads = call(
        dense_kernel,
        [shape(NZL, H + NX * share, T)],
        [VMEM] * 3,
        flops=2 * T * H * H,
        name="dense",
    )(part, weight, grad_out)
    with jax.named_scope("gather_gradients"):
        grads = exchange(grads, "zl")
        common = jnp.broadcast_to(grads[None, :, :H], (NX, NZL, H, T))
        slices = grads[:, H:].reshape(NZL, NX, share, T).transpose(1, 0, 2, 3)
        grads = exchange(jnp.concatenate([common, slices], axis=2), "x")
        grads = grads.reshape(row_tiles, H + share, T)
    mine, theirs = call(
        backward_kernel,
        [shape(half * H + pair_rows, T), shape(half * H + pair_rows, T)],
        [SMEM, SMEM, VMEM, VMEM, VMEM],
        flops=product_flops,
        scratch=[VMEM((row_tiles, H, T), BF16), VMEM((col_tiles, H, T), F32)],
        name="backward_products",
    )(coord_set, core, tile_set, grads, weight)
    with jax.named_scope("sum_over_row"):
        theirs = swap_cores(theirs)
        back = call(core_sum_kernel, [shape(NY, NZH * H + pair_rows, T)], [VMEM] * 2, name="core_sum")(
            mine, theirs
        )
        back = exchange(back, "y")
        back = call(y_sum_kernel, [shape(NZH, H + pair_rows, T)], [VMEM], name="y_sum")(back)
        back = exchange(back, "zh")
        grad_features, weight_grad = call(
            last_sum_kernel, [shape(T, H), shape(row_tiles, share, H, dtype=F32)], [VMEM], name="last_sum"
        )(back)
    with jax.named_scope("gather_weight_grad"):
        weight_grad = exchange(weight_grad, COL).reshape(H, H)
    return grad_features, weight_grad


def solution(mesh):
    fine = Mesh(mesh.devices.reshape(tuple(SIZES.values())), tuple(SIZES))
    in_specs = (
        P(COL + ROW, None),
        P(ROW + COL, None),
        P(),
        P(ROW, COL, None, None, None),
        P(ROW, COL, None, None),
    )
    out_specs = (P(COL + ROW, None), P())
    return jax.shard_map(
        on_device, mesh=fine, in_specs=in_specs, out_specs=out_specs, check_vma=False
    )
```

```python
import math

import jax
import jax.numpy as jnp
from jax import lax
from jax.experimental import pallas as pl
from jax.experimental.pallas import tpu as pltpu
from jax.sharding import Mesh
from jax.sharding import PartitionSpec as P

F32 = jnp.float32
BF16 = jnp.bfloat16
SIZES = {"y": 4, "zh": 4, "co": 2, "x": 4, "zl": 4}
NY, NZH, NCO, NX, NZL = (SIZES[a] for a in ("y", "zh", "co", "x", "zl"))
N = 4
FAR = N - 1
ROW = ("y", "zh", "co")
COL = ("x", "zl")
T = 128
H = 256
GROUP = 32
VMEM_LIMIT = 20 * 1024 * 1024
VMEM_MOST = 48 * 1024 * 1024


def exchange(value, axis):
    return lax.all_to_all(value, axis, 0, 0, tiled=True)


def spread(value, axis):
    return exchange(jnp.broadcast_to(value[None], (SIZES[axis],) + value.shape), axis)


def swap_cores(value):
    return lax.ppermute(value, "co", [(0, 1), (1, 0)])


def shift(value, axis, distance):
    n = SIZES[axis]
    return lax.ppermute(value, axis, [(i, (i + distance) % n) for i in range(n)])


def place(ahead_y, ahead_zh):
    return jnp.where(ahead_zh == 0, ahead_y, FAR + FAR * ahead_y + ahead_zh)


def split_pair(value):
    high = value.astype(BF16)
    low = (value - high.astype(F32)).astype(BF16)
    return jnp.concatenate([high[:, :T], high[:, T:], low[:, :T], low[:, T:]], axis=0)


def join_pair(rows):
    n = rows.shape[0] // 4
    rows = rows.astype(F32)
    high = jnp.concatenate([rows[:n], rows[n : 2 * n]], axis=1)
    low = jnp.concatenate([rows[2 * n : 3 * n], rows[3 * n :]], axis=1)
    return high + low


def far_copies_kernel(zh, gathered, near1, near2, near3, out_near, out_far):
    for d in range(1, N):
        block = gathered[(zh[0] - d) & FAR]
        for y in range(N):
            out_far[y, d - 1] = block
    out_near[0] = gathered[zh[0]]
    for y, near in enumerate((near1, near2, near3), 1):
        out_near[y] = near[...]


def forward_kernel(
    coords, core, y, zh, tiles_hbm, near, far, near_other, far_other, out, tiles, source, total, arrived
):
    groups = tiles.shape[0] // GROUP

    def fetch(g):
        at = pl.ds(g * GROUP, GROUP)
        return pltpu.make_async_copy(tiles_hbm.at[at], tiles.at[at], arrived.at[g])

    for g in range(groups):
        fetch(g).start()
    half = source.shape[0] // 2
    for c, (a, b) in enumerate(((near, far), (near_other, far_other))):
        first = c * half
        source[first : first + N] = a[...]
        for i in range(N):
            at = first + N + i * FAR
            source[at : at + FAR] = b[i]
    total[...] = jnp.zeros_like(total)
    me, my_y, my_zh = core[0], y[0], zh[0]

    def step(g, carry):
        fetch(g).wait()
        products = []
        for u in range(GROUP):
            k = g * GROUP + u
            j = coords[2 * k + 1]
            ahead = (my_zh - (j >> 1)) & FAR
            behind_y = jnp.where(ahead == 0, (my_y - (j >> 3)) & FAR, j >> 3)
            at = ((j & 1) ^ me) * half + place(behind_y, ahead)
            products.append(jnp.dot(tiles[k], source[at], preferred_element_type=F32))
        for u in range(GROUP):
            i = coords[2 * (g * GROUP + u)]
            total[i] += products[u]
        return carry

    lax.fori_loop(0, groups, step, 0)
    out[...] = total[...].astype(out.dtype)


def x_sum_kernel(parts, out):
    total = parts[0].astype(F32)
    for s in range(1, parts.shape[0]):
        total = total + parts[s].astype(F32)
    out[...] = total.astype(BF16)


def dense_kernel(parts, weight, grad_out, out):
    total = parts[0].astype(F32)
    for s in range(1, parts.shape[0]):
        total = total + parts[s].astype(F32)
    aggregated = total.astype(BF16)
    pre = jnp.dot(aggregated, weight[...], preferred_element_type=F32)
    sig = jax.nn.sigmoid(pre)
    slope = grad_out[...].astype(F32) * (sig * (1.0 + pre * (1.0 - sig)))
    slope_t = slope.T.astype(BF16)
    agg_t = aggregated.astype(F32).T.astype(BF16)
    share = H // (NX * NZL)
    for l in range(NZL):
        out[l, :H] = slope_t
        for x in range(NX):
            at = (x * NZL + l) * share
            out[l, H + x * share : H + (x + 1) * share] = agg_t[at : at + share]


def backward_kernel(
    coords, core, y, zh, tiles, grads, weight, mine_near, mine_far, other_near, other_far, source, total
):
    blocks = grads.shape[0]
    half = total.shape[0] // 2
    total[...] = jnp.zeros_like(total)
    me, my_y, my_zh = core[0], y[0], zh[0]
    share = grads.shape[1] - H
    weight_grad = jnp.zeros((share, H), F32)
    for c in range(blocks):
        slope_t = grads[c, :H]
        source[c] = jnp.dot(weight[...], slope_t, preferred_element_type=F32).astype(BF16)
        weight_grad = weight_grad + lax.dot_general(
            grads[c, H:], slope_t, (((1,), (1,)), ((), ())), preferred_element_type=F32
        )

    def step(g, carry):
        products = []
        for u in range(GROUP):
            k = g * GROUP + u
            products.append(jnp.dot(source[coords[2 * k]], tiles[k], preferred_element_type=F32))
        for u in range(GROUP):
            j = coords[2 * (g * GROUP + u) + 1]
            ahead = ((j >> 1) - my_zh) & FAR
            ahead_y = jnp.where(ahead == 0, ((j >> 3) - my_y) & FAR, j >> 3)
            at = ((j & 1) ^ me) * half + place(ahead_y, ahead)
            total[at] += products[u]
        return carry

    lax.fori_loop(0, tiles.shape[0] // GROUP, step, 0)
    pair = split_pair(weight_grad)
    rows = FAR * H
    for first, near, far in ((0, mine_near, mine_far), (half, other_near, other_far)):
        for i in range(N):
            near[i] = total[first + i].astype(BF16)
            for d in range(FAR):
                at = i * rows + d * H
                far[at : at + H] = total[first + N + i * FAR + d].astype(BF16)
        far[N * rows :] = pair


def core_sum_kernel(mine, other, out):
    rows = FAR * H
    pair = split_pair(join_pair(mine[N * rows :]) + join_pair(other[N * rows :]))
    for y in range(N):
        at = pl.ds(y * rows, rows)
        out[y, :rows] = (mine[at].astype(F32) + other[at].astype(F32)).astype(BF16)
        out[y, rows:] = pair


def near_sum_kernel(mine, other, *outs):
    for d, out in enumerate(outs):
        out[...] = (mine[d].astype(F32) + other[d].astype(F32)).astype(BF16)


def y_sum_kernel(zh, parts, out):
    rows = FAR * H
    grad = join_pair(parts[0, rows:])
    for s in range(1, N):
        grad = grad + join_pair(parts[s, rows:])
    grad = jnp.concatenate([grad[:, :T], grad[:, T:]], axis=0).astype(BF16)
    for d in range(N):
        to = (zh[0] + d) & FAR
        if d == 0:
            out[to, :H] = jnp.zeros((H, T), BF16)
        else:
            at = pl.ds((d - 1) * H, H)
            total = parts[0, at].astype(F32)
            for s in range(1, N):
                total = total + parts[s, at].astype(F32)
            out[to, :H] = total.astype(BF16)
        out[to, H:] = grad


def last_sum_kernel(parts, near0, near1, near2, near3, out, weight_grad):
    total = near0[...].astype(F32)
    for near in (near1, near2, near3):
        total = total + near[...].astype(F32)
    grad = jnp.zeros((parts.shape[1] - H, T), F32)
    for s in range(N):
        total = total + parts[s, :H].astype(F32)
        grad = grad + parts[s, H:].astype(F32)
    out[...] = total.T.astype(BF16)
    share = grad.shape[0] // 2
    scale = 1.0 / math.sqrt(T * math.prod(SIZES.values()))
    grad = jnp.concatenate([grad[:share], grad[share:]], axis=1) * scale
    for c in range(NX * NZL):
        weight_grad[c] = grad.astype(BF16)


def shape(*dims, dtype=BF16):
    return jax.ShapeDtypeStruct(dims, dtype)


def call(body, outs, ins, flops=0, scratch=(), name=None, limit=VMEM_LIMIT):
    moved = sum(math.prod(o.shape) * o.dtype.itemsize for o in outs)
    single = len(outs) == 1
    vmem = pl.BlockSpec(memory_space=pltpu.VMEM)
    return pl.pallas_call(
        body,
        out_shape=outs[0] if single else tuple(outs),
        in_specs=[pl.BlockSpec(memory_space=s) for s in ins],
        out_specs=vmem if single else tuple(vmem for _ in outs),
        scratch_shapes=list(scratch),
        compiler_params=pltpu.CompilerParams(vmem_limit_bytes=limit),
        cost_estimate=pl.CostEstimate(flops=flops, bytes_accessed=4 * moved, transcendentals=0),
        name=name,
    )


def on_device(features, grad_out, weight, tiles, coords):
    tile_set = tiles[0, 0]
    coord_set = coords[0, 0].reshape(-1)
    slots = tile_set.shape[0]
    core, y, zh = (lax.axis_index(a).astype(jnp.int32).reshape(1) for a in ("co", "y", "zh"))
    row_tiles, col_tiles = NX * NZL, NY * NZH * NCO
    share = H // row_tiles
    pair_rows = 4 * share
    SMEM, VMEM = pltpu.SMEM, pltpu.VMEM
    product_flops = 2 * slots * T * T * H

    with jax.named_scope("gather_features"):
        gathered = spread(features, "zh").reshape(N, T, H)
        near = [shift(features, "y", d) for d in range(1, N)]
        near, far = call(
            far_copies_kernel,
            [shape(N, T, H), shape(N, FAR, T, H)],
            [SMEM] + [VMEM] * N,
            name="far_copies",
        )(zh, gathered, *near)
        near_other = swap_cores(near)
        far = exchange(far, "y")
        near_other, far = lax.optimization_barrier((near_other, far))
        far_other = swap_cores(far)
    part = call(
        forward_kernel,
        [shape(row_tiles, T, H)],
        [SMEM] * 4 + [pltpu.HBM] + [VMEM] * 4,
        flops=product_flops,
        scratch=[
            VMEM((slots, T, T), BF16),
            VMEM((col_tiles, T, H), BF16),
            VMEM((row_tiles, T, H), F32),
            pltpu.SemaphoreType.DMA((slots // GROUP,)),
        ],
        name="forward_products",
        limit=VMEM_MOST,
    )(coord_set, core, y, zh, tile_set, near, far, near_other, far_other)
    with jax.named_scope("sum_over_col"):
        part = exchange(part.reshape(NX, NZL, T, H), "x")
        part = call(x_sum_kernel, [shape(NZL, T, H)], [VMEM], name="x_sum")(part)
        part = exchange(part, "zl")
    grads = call(
        dense_kernel,
        [shape(NZL, H + NX * share, T)],
        [VMEM] * 3,
        flops=2 * T * H * H,
        name="dense",
    )(part, weight, grad_out)
    with jax.named_scope("gather_gradients"):
        grads = exchange(grads, "zl")
        common = jnp.broadcast_to(grads[None, :, :H], (NX, NZL, H, T))
        slices = grads[:, H:].reshape(NZL, NX, share, T).transpose(1, 0, 2, 3)
        grads = exchange(jnp.concatenate([common, slices], axis=2), "x")
        grads = grads.reshape(row_tiles, H + share, T)
    rows = FAR * H
    outs = [shape(N, H, T), shape(N * rows + pair_rows, T)]
    mine_near, mine_far, other_near, other_far = call(
        backward_kernel,
        outs + outs,
        [SMEM] * 4 + [VMEM] * 3,
        flops=product_flops,
        scratch=[VMEM((row_tiles, H, T), BF16), VMEM((col_tiles, H, T), F32)],
        name="backward_products",
    )(coord_set, core, y, zh, tile_set, grads, weight)
    with jax.named_scope("sum_over_row"):
        other_far = swap_cores(other_far)
        far = call(core_sum_kernel, [shape(N, rows + pair_rows, T)], [VMEM] * 2, name="core_sum")(mine_far, other_far)
        far = exchange(far, "y")
        other_near = swap_cores(other_near)
        near = call(near_sum_kernel, [shape(H, T)] * N, [VMEM] * 2, name="near_sum")(mine_near, other_near)
        far = call(y_sum_kernel, [shape(N, H + 2 * share, T)], [SMEM, VMEM], name="y_sum")(zh, far)
        far = exchange(far, "zh")
        near = [near[0]] + [shift(near[d], "y", d) for d in range(1, N)]
        grad_features, weight_grad = call(
            last_sum_kernel,
            [shape(T, H), shape(row_tiles, share, H)],
            [VMEM] * 5,
            name="last_sum",
        )(far, *near)
    with jax.named_scope("gather_weight_grad"):
        weight_grad = exchange(weight_grad, COL).reshape(H, H).astype(F32)
    return grad_features, weight_grad


def solution(mesh):
    fine = Mesh(mesh.devices.reshape(tuple(SIZES.values())), tuple(SIZES))
    in_specs = (
        P(COL + ROW, None),
        P(ROW + COL, None),
        P(),
        P(ROW, COL, None, None, None),
        P(ROW, COL, None, None),
    )
    out_specs = (P(COL + ROW, None), P())
    return jax.shard_map(
        on_device, mesh=fine, in_specs=in_specs, out_specs=out_specs, check_vma=False
    )
```

```python
import math

import jax
import jax.numpy as jnp
from jax import lax
from jax.experimental import pallas as pl
from jax.experimental.pallas import tpu as pltpu
from jax.sharding import Mesh
from jax.sharding import PartitionSpec as P

F32 = jnp.float32
BF16 = jnp.bfloat16
SIZES = {"y": 4, "zh": 4, "co": 2, "x": 4, "zl": 4}
NY, NZH, NCO, NX, NZL = (SIZES[a] for a in ("y", "zh", "co", "x", "zl"))
N = 4
FAR = N - 1
ROW = ("y", "zh", "co")
COL = ("x", "zl")
T = 128
H = 256
GROUP = 32
VMEM_LIMIT = 20 * 1024 * 1024
VMEM_MOST = 48 * 1024 * 1024


def exchange(value, axis):
    return lax.all_to_all(value, axis, 0, 0, tiled=True)


def spread(value, axis):
    return exchange(jnp.broadcast_to(value[None], (SIZES[axis],) + value.shape), axis)


def swap_cores(value):
    return lax.ppermute(value, "co", [(0, 1), (1, 0)])


def shift(value, axis, distance):
    n = SIZES[axis]
    return lax.ppermute(value, axis, [(i, (i + distance) % n) for i in range(n)])


def place(ahead_y, ahead_zh):
    return jnp.where(ahead_zh == 0, ahead_y, FAR + FAR * ahead_y + ahead_zh)


def split_pair(value):
    high = value.astype(BF16)
    low = (value - high.astype(F32)).astype(BF16)
    return jnp.concatenate([high[:, :T], high[:, T:], low[:, :T], low[:, T:]], axis=0)


def join_pair(rows):
    n = rows.shape[0] // 4
    rows = rows.astype(F32)
    high = jnp.concatenate([rows[:n], rows[n : 2 * n]], axis=1)
    low = jnp.concatenate([rows[2 * n : 3 * n], rows[3 * n :]], axis=1)
    return high + low


def far_copies_kernel(zh, gathered, near1, near2, near3, out_near, out_far):
    for d in range(1, N):
        block = gathered[(zh[0] - d) & FAR]
        for y in range(N):
            out_far[y, d - 1] = block
    out_near[0] = gathered[zh[0]]
    for y, near in enumerate((near1, near2, near3), 1):
        out_near[y] = near[...]


def forward_kernel(
    coords, core, y, zh, tiles_hbm, near, far, near_other, far_other, out, tiles, source, total, arrived
):
    groups = tiles.shape[0] // GROUP

    def fetch(g):
        at = pl.ds(g * GROUP, GROUP)
        return pltpu.make_async_copy(tiles_hbm.at[at], tiles.at[at], arrived.at[g])

    for g in range(groups):
        fetch(g).start()
    half = source.shape[0] // 2
    for c, (a, b) in enumerate(((near, far), (near_other, far_other))):
        first = c * half
        source[first : first + N] = a[...]
        for i in range(N):
            at = first + N + i * FAR
            source[at : at + FAR] = b[i]
    total[...] = jnp.zeros_like(total)
    me, my_y, my_zh = core[0], y[0], zh[0]

    def step(g, carry):
        fetch(g).wait()
        products = []
        for u in range(GROUP):
            k = g * GROUP + u
            j = coords[2 * k + 1]
            ahead = (my_zh - (j >> 1)) & FAR
            behind_y = jnp.where(ahead == 0, (my_y - (j >> 3)) & FAR, j >> 3)
            at = ((j & 1) ^ me) * half + place(behind_y, ahead)
            products.append(jnp.dot(tiles[k], source[at], preferred_element_type=F32))
        for u in range(GROUP):
            i = coords[2 * (g * GROUP + u)]
            total[i] += products[u]
        return carry

    lax.fori_loop(0, groups, step, 0)
    out[...] = total[...].astype(out.dtype)


def x_sum_kernel(parts, out):
    total = parts[0].astype(F32)
    for s in range(1, parts.shape[0]):
        total = total + parts[s].astype(F32)
    out[...] = total.astype(BF16)


def dense_kernel(parts, weight, grad_out, out):
    total = parts[0].astype(F32)
    for s in range(1, parts.shape[0]):
        total = total + parts[s].astype(F32)
    aggregated = total.astype(BF16)
    pre = jnp.dot(aggregated, weight[...], preferred_element_type=F32)
    sig = jax.nn.sigmoid(pre)
    slope = grad_out[...].astype(F32) * (sig * (1.0 + pre * (1.0 - sig)))
    slope_t = slope.T.astype(BF16)
    agg_t = aggregated.astype(F32).T.astype(BF16)
    share = H // (NX * NZL)
    for l in range(NZL):
        out[l, :H] = slope_t
        for x in range(NX):
            at = (x * NZL + l) * share
            out[l, H + x * share : H + (x + 1) * share] = agg_t[at : at + share]


def backward_kernel(
    coords, core, y, zh, tiles, grads, weight, mine_near, mine_far, other_near, other_far, source, total
):
    blocks = grads.shape[0]
    half = total.shape[0] // 2
    total[...] = jnp.zeros_like(total)
    me, my_y, my_zh = core[0], y[0], zh[0]
    share = grads.shape[1] - H
    weight_grad = jnp.zeros((share, H), F32)
    for c in range(blocks):
        slope_t = grads[c, :H]
        source[c] = jnp.dot(weight[...], slope_t, preferred_element_type=F32).astype(BF16)
        weight_grad = weight_grad + lax.dot_general(
            grads[c, H:], slope_t, (((1,), (1,)), ((), ())), preferred_element_type=F32
        )

    def step(g, carry):
        products = []
        for u in range(GROUP):
            k = g * GROUP + u
            products.append(jnp.dot(source[coords[2 * k]], tiles[k], preferred_element_type=F32))
        for u in range(GROUP):
            j = coords[2 * (g * GROUP + u) + 1]
            ahead = ((j >> 1) - my_zh) & FAR
            ahead_y = jnp.where(ahead == 0, ((j >> 3) - my_y) & FAR, j >> 3)
            at = ((j & 1) ^ me) * half + place(ahead_y, ahead)
            total[at] += products[u]
        return carry

    lax.fori_loop(0, tiles.shape[0] // GROUP, step, 0)
    pair = split_pair(weight_grad * (1.0 / math.sqrt(T * math.prod(SIZES.values()))))
    rows = FAR * H
    for first, near, far in ((0, mine_near, mine_far), (half, other_near, other_far)):
        for i in range(N):
            near[i] = total[first + i].astype(BF16)
            for d in range(FAR):
                at = i * rows + d * H
                far[at : at + H] = total[first + N + i * FAR + d].astype(BF16)
        far[N * rows :] = pair


def core_sum_kernel(mine, other, out):
    rows = FAR * H
    pair = split_pair(join_pair(mine[N * rows :]) + join_pair(other[N * rows :]))
    for y in range(N):
        at = pl.ds(y * rows, rows)
        out[y, :rows] = (mine[at].astype(F32) + other[at].astype(F32)).astype(BF16)
        out[y, rows:] = pair


def near_sum_kernel(mine, other, *outs):
    for d, out in enumerate(outs):
        out[...] = (mine[d].astype(F32) + other[d].astype(F32)).astype(BF16)


def y_sum_kernel(zh, parts, out):
    rows = FAR * H
    grad = join_pair(parts[0, rows:])
    for s in range(1, N):
        grad = grad + join_pair(parts[s, rows:])
    grad = jnp.concatenate([grad[:, :T], grad[:, T:]], axis=0).astype(BF16)
    for d in range(N):
        to = (zh[0] + d) & FAR
        if d == 0:
            out[to, :H] = jnp.zeros((H, T), BF16)
        else:
            at = pl.ds((d - 1) * H, H)
            total = parts[0, at].astype(F32)
            for s in range(1, N):
                total = total + parts[s, at].astype(F32)
            out[to, :H] = total.astype(BF16)
        out[to, H:] = grad


def last_sum_kernel(parts, near0, near1, near2, near3, out, weight_grad):
    total = near0[...].astype(F32)
    for near in (near1, near2, near3):
        total = total + near[...].astype(F32)
    grad = jnp.zeros((parts.shape[1] - H, T), F32)
    for s in range(N):
        total = total + parts[s, :H].astype(F32)
        grad = grad + parts[s, H:].astype(F32)
    out[...] = total.T.astype(BF16)
    share = grad.shape[0] // 2
    grad = jnp.concatenate([grad[:share], grad[share:]], axis=1)
    for c in range(NX * NZL):
        weight_grad[c] = grad.astype(BF16)


def shape(*dims, dtype=BF16):
    return jax.ShapeDtypeStruct(dims, dtype)


def call(body, outs, ins, flops=0, scratch=(), name=None, limit=VMEM_LIMIT):
    moved = sum(math.prod(o.shape) * o.dtype.itemsize for o in outs)
    single = len(outs) == 1
    vmem = pl.BlockSpec(memory_space=pltpu.VMEM)
    return pl.pallas_call(
        body,
        out_shape=outs[0] if single else tuple(outs),
        in_specs=[pl.BlockSpec(memory_space=s) for s in ins],
        out_specs=vmem if single else tuple(vmem for _ in outs),
        scratch_shapes=list(scratch),
        compiler_params=pltpu.CompilerParams(vmem_limit_bytes=limit),
        cost_estimate=pl.CostEstimate(flops=flops, bytes_accessed=4 * moved, transcendentals=0),
        name=name,
    )


def on_device(features, grad_out, weight, tiles, coords):
    tile_set = tiles[0, 0]
    coord_set = coords[0, 0].reshape(-1)
    slots = tile_set.shape[0]
    core, y, zh = (lax.axis_index(a).astype(jnp.int32).reshape(1) for a in ("co", "y", "zh"))
    row_tiles, col_tiles = NX * NZL, NY * NZH * NCO
    share = H // row_tiles
    pair_rows = 4 * share
    SMEM, VMEM = pltpu.SMEM, pltpu.VMEM
    product_flops = 2 * slots * T * T * H

    with jax.named_scope("gather_features"):
        gathered = spread(features, "zh").reshape(N, T, H)
        near = [shift(features, "y", d) for d in range(1, N)]
        near, far = call(
            far_copies_kernel,
            [shape(N, T, H), shape(N, FAR, T, H)],
            [SMEM] + [VMEM] * N,
            name="far_copies",
        )(zh, gathered, *near)
        near_other = swap_cores(near)
        far = exchange(far, "y")
        near_other, far = lax.optimization_barrier((near_other, far))
        far_other = swap_cores(far)
    part = call(
        forward_kernel,
        [shape(row_tiles, T, H)],
        [SMEM] * 4 + [pltpu.HBM] + [VMEM] * 4,
        flops=product_flops,
        scratch=[
            VMEM((slots, T, T), BF16),
            VMEM((col_tiles, T, H), BF16),
            VMEM((row_tiles, T, H), F32),
            pltpu.SemaphoreType.DMA((slots // GROUP,)),
        ],
        name="forward_products",
        limit=VMEM_MOST,
    )(coord_set, core, y, zh, tile_set, near, far, near_other, far_other)
    with jax.named_scope("sum_over_col"):
        part = exchange(part.reshape(NX, NZL, T, H), "x")
        part = call(x_sum_kernel, [shape(NZL, T, H)], [VMEM], name="x_sum")(part)
        part = exchange(part, "zl")
    grads = call(
        dense_kernel,
        [shape(NZL, H + NX * share, T)],
        [VMEM] * 3,
        flops=2 * T * H * H,
        name="dense",
    )(part, weight, grad_out)
    with jax.named_scope("gather_gradients"):
        grads = exchange(grads, "zl")
        common = jnp.broadcast_to(grads[None, :, :H], (NX, NZL, H, T))
        slices = grads[:, H:].reshape(NZL, NX, share, T).transpose(1, 0, 2, 3)
        grads = exchange(jnp.concatenate([common, slices], axis=2), "x")
        grads = grads.reshape(row_tiles, H + share, T)
    rows = FAR * H
    outs = [shape(N, H, T), shape(N * rows + pair_rows, T)]
    mine_near, mine_far, other_near, other_far = call(
        backward_kernel,
        outs + outs,
        [SMEM] * 4 + [VMEM] * 3,
        flops=product_flops,
        scratch=[VMEM((row_tiles, H, T), BF16), VMEM((col_tiles, H, T), F32)],
        name="backward_products",
    )(coord_set, core, y, zh, tile_set, grads, weight)
    with jax.named_scope("sum_over_row"):
        other_far = swap_cores(other_far)
        far = call(core_sum_kernel, [shape(N, rows + pair_rows, T)], [VMEM] * 2, name="core_sum")(mine_far, other_far)
        far = exchange(far, "y")
        other_near = swap_cores(other_near)
        near = call(near_sum_kernel, [shape(H, T)] * N, [VMEM] * 2, name="near_sum")(mine_near, other_near)
        far = call(y_sum_kernel, [shape(N, H + 2 * share, T)], [SMEM, VMEM], name="y_sum")(zh, far)
        far = exchange(far, "zh")
        near = [near[0]] + [shift(near[d], "y", d) for d in range(1, N)]
        grad_features, weight_grad = call(
            last_sum_kernel,
            [shape(T, H), shape(row_tiles, share, H)],
            [VMEM] * 5,
            name="last_sum",
        )(far, *near)
    with jax.named_scope("gather_weight_grad"):
        weight_grad = exchange(weight_grad, COL).reshape(H, H).astype(F32)
    return grad_features, weight_grad


def solution(mesh):
    fine = Mesh(mesh.devices.reshape(tuple(SIZES.values())), tuple(SIZES))
    in_specs = (
        P(COL + ROW, None),
        P(ROW + COL, None),
        P(),
        P(ROW, COL, None, None, None),
        P(ROW, COL, None, None),
    )
    out_specs = (P(COL + ROW, None), P())
    return jax.shard_map(
        on_device, mesh=fine, in_specs=in_specs, out_specs=out_specs, check_vma=False
    )
```

```python
import math

import jax
import jax.numpy as jnp
from jax import lax
from jax.experimental import pallas as pl
from jax.experimental.pallas import tpu as pltpu
from jax.sharding import Mesh
from jax.sharding import PartitionSpec as P

F32 = jnp.float32
BF16 = jnp.bfloat16
SIZES = {"y": 4, "zh": 4, "co": 2, "x": 4, "zl": 4}
NY, NZH, NCO, NX, NZL = (SIZES[a] for a in ("y", "zh", "co", "x", "zl"))
N = 4
FAR = N - 1
ROW = ("y", "zh", "co")
COL = ("x", "zl")
T = 128
H = 256
GROUP = 32
BACK_GROUP = 48
VMEM_LIMIT = 20 * 1024 * 1024
VMEM_MOST = 48 * 1024 * 1024


def exchange(value, axis):
    return lax.all_to_all(value, axis, 0, 0, tiled=True)


def spread(value, axis):
    return exchange(jnp.broadcast_to(value[None], (SIZES[axis],) + value.shape), axis)


def swap_cores(value):
    return lax.ppermute(value, "co", [(0, 1), (1, 0)])


def shift(value, axis, distance):
    n = SIZES[axis]
    return lax.ppermute(value, axis, [(i, (i + distance) % n) for i in range(n)])


def place(ahead_y, ahead_zh):
    return jnp.where(ahead_zh == 0, ahead_y, FAR + FAR * ahead_y + ahead_zh)


def split_pair(value):
    high = value.astype(BF16)
    low = (value - high.astype(F32)).astype(BF16)
    return jnp.concatenate([high[:, :T], high[:, T:], low[:, :T], low[:, T:]], axis=0)


def join_pair(rows):
    n = rows.shape[0] // 4
    rows = rows.astype(F32)
    high = jnp.concatenate([rows[:n], rows[n : 2 * n]], axis=1)
    low = jnp.concatenate([rows[2 * n : 3 * n], rows[3 * n :]], axis=1)
    return high + low


def far_copies_kernel(zh, gathered, near1, near2, near3, out_near, out_far):
    for d in range(1, N):
        block = gathered[(zh[0] - d) & FAR]
        for y in range(N):
            out_far[y, d - 1] = block
    out_near[0] = gathered[zh[0]]
    for y, near in enumerate((near1, near2, near3), 1):
        out_near[y] = near[...]


def forward_kernel(
    coords, core, y, zh, tiles_hbm, near, far, near_other, far_other, out, tiles, source, total, arrived
):
    groups = tiles.shape[0] // GROUP

    def fetch(g):
        at = pl.ds(g * GROUP, GROUP)
        return pltpu.make_async_copy(tiles_hbm.at[at], tiles.at[at], arrived.at[g])

    for g in range(groups):
        fetch(g).start()
    half = source.shape[0] // 2
    for c, (a, b) in enumerate(((near, far), (near_other, far_other))):
        first = c * half
        source[first : first + N] = a[...]
        for i in range(N):
            at = first + N + i * FAR
            source[at : at + FAR] = b[i]
    total[...] = jnp.zeros_like(total)
    me, my_y, my_zh = core[0], y[0], zh[0]

    def step(g, carry):
        fetch(g).wait()
        products = []
        for u in range(GROUP):
            k = g * GROUP + u
            j = coords[2 * k + 1]
            ahead = (my_zh - (j >> 1)) & FAR
            behind_y = jnp.where(ahead == 0, (my_y - (j >> 3)) & FAR, j >> 3)
            at = ((j & 1) ^ me) * half + place(behind_y, ahead)
            products.append(jnp.dot(tiles[k], source[at], preferred_element_type=F32))
        for u in range(GROUP):
            i = coords[2 * (g * GROUP + u)]
            total[i] += products[u]
        return carry

    lax.fori_loop(0, groups, step, 0)
    out[...] = total[...].astype(out.dtype)


def x_sum_kernel(parts, out):
    total = parts[0].astype(F32)
    for s in range(1, parts.shape[0]):
        total = total + parts[s].astype(F32)
    out[...] = total.astype(BF16)


def dense_kernel(parts, weight, grad_out, out):
    total = parts[0].astype(F32)
    for s in range(1, parts.shape[0]):
        total = total + parts[s].astype(F32)
    aggregated = total.astype(BF16)
    pre = jnp.dot(aggregated, weight[...], preferred_element_type=F32)
    sig = jax.nn.sigmoid(pre)
    slope = grad_out[...].astype(F32) * (sig * (1.0 + pre * (1.0 - sig)))
    slope_t = slope.T.astype(BF16)
    agg_t = aggregated.astype(F32).T.astype(BF16)
    share = H // (NX * NZL)
    for l in range(NZL):
        out[l, :H] = slope_t
        for x in range(NX):
            at = (x * NZL + l) * share
            out[l, H + x * share : H + (x + 1) * share] = agg_t[at : at + share]


def backward_kernel(
    coords, core, y, zh, tiles, grads, weight, mine_near, mine_far, other_near, other_far, source, total
):
    blocks = grads.shape[0]
    half = total.shape[0] // 2
    total[...] = jnp.zeros_like(total)
    me, my_y, my_zh = core[0], y[0], zh[0]
    share = grads.shape[1] - H
    weight_grad = jnp.zeros((share, H), F32)
    for c in range(blocks):
        slope_t = grads[c, :H]
        source[c] = jnp.dot(weight[...], slope_t, preferred_element_type=F32).astype(BF16)
        weight_grad = weight_grad + lax.dot_general(
            grads[c, H:], slope_t, (((1,), (1,)), ((), ())), preferred_element_type=F32
        )

    def step(g, carry):
        products = []
        for u in range(BACK_GROUP):
            k = g * BACK_GROUP + u
            products.append(jnp.dot(source[coords[2 * k]], tiles[k], preferred_element_type=F32))
        for u in range(BACK_GROUP):
            j = coords[2 * (g * BACK_GROUP + u) + 1]
            ahead = ((j >> 1) - my_zh) & FAR
            ahead_y = jnp.where(ahead == 0, ((j >> 3) - my_y) & FAR, j >> 3)
            at = ((j & 1) ^ me) * half + place(ahead_y, ahead)
            total[at] += products[u]
        return carry

    lax.fori_loop(0, tiles.shape[0] // BACK_GROUP, step, 0)
    pair = split_pair(weight_grad * (1.0 / math.sqrt(T * math.prod(SIZES.values()))))
    rows = FAR * H
    for first, near, far in ((0, mine_near, mine_far), (half, other_near, other_far)):
        for i in range(N):
            near[i] = total[first + i].astype(BF16)
            for d in range(FAR):
                at = i * rows + d * H
                far[at : at + H] = total[first + N + i * FAR + d].astype(BF16)
        far[N * rows :] = pair


def core_sum_kernel(mine, other, out):
    rows = FAR * H
    pair = split_pair(join_pair(mine[N * rows :]) + join_pair(other[N * rows :]))
    for y in range(N):
        at = pl.ds(y * rows, rows)
        out[y, :rows] = (mine[at].astype(F32) + other[at].astype(F32)).astype(BF16)
        out[y, rows:] = pair


def near_sum_kernel(mine, other, *outs):
    for d, out in enumerate(outs):
        out[...] = (mine[d].astype(F32) + other[d].astype(F32)).astype(BF16)


def y_sum_kernel(zh, parts, out):
    rows = FAR * H
    grad = join_pair(parts[0, rows:])
    for s in range(1, N):
        grad = grad + join_pair(parts[s, rows:])
    grad = jnp.concatenate([grad[:, :T], grad[:, T:]], axis=0).astype(BF16)
    for d in range(N):
        to = (zh[0] + d) & FAR
        if d == 0:
            out[to, :H] = jnp.zeros((H, T), BF16)
        else:
            at = pl.ds((d - 1) * H, H)
            total = parts[0, at].astype(F32)
            for s in range(1, N):
                total = total + parts[s, at].astype(F32)
            out[to, :H] = total.astype(BF16)
        out[to, H:] = grad


def last_sum_kernel(parts, near0, near1, near2, near3, out, weight_grad):
    total = near0[...].astype(F32)
    for near in (near1, near2, near3):
        total = total + near[...].astype(F32)
    grad = jnp.zeros((parts.shape[1] - H, T), F32)
    for s in range(N):
        total = total + parts[s, :H].astype(F32)
        grad = grad + parts[s, H:].astype(F32)
    out[...] = total.T.astype(BF16)
    share = grad.shape[0] // 2
    grad = jnp.concatenate([grad[:share], grad[share:]], axis=1)
    for c in range(NX * NZL):
        weight_grad[c] = grad.astype(BF16)


def shape(*dims, dtype=BF16):
    return jax.ShapeDtypeStruct(dims, dtype)


def call(body, outs, ins, flops=0, scratch=(), name=None, limit=VMEM_LIMIT):
    moved = sum(math.prod(o.shape) * o.dtype.itemsize for o in outs)
    single = len(outs) == 1
    vmem = pl.BlockSpec(memory_space=pltpu.VMEM)
    return pl.pallas_call(
        body,
        out_shape=outs[0] if single else tuple(outs),
        in_specs=[pl.BlockSpec(memory_space=s) for s in ins],
        out_specs=vmem if single else tuple(vmem for _ in outs),
        scratch_shapes=list(scratch),
        compiler_params=pltpu.CompilerParams(vmem_limit_bytes=limit),
        cost_estimate=pl.CostEstimate(flops=flops, bytes_accessed=4 * moved, transcendentals=0),
        name=name,
    )


def on_device(features, grad_out, weight, tiles, coords):
    tile_set = tiles[0, 0]
    coord_set = coords[0, 0].reshape(-1)
    slots = tile_set.shape[0]
    core, y, zh = (lax.axis_index(a).astype(jnp.int32).reshape(1) for a in ("co", "y", "zh"))
    row_tiles, col_tiles = NX * NZL, NY * NZH * NCO
    share = H // row_tiles
    pair_rows = 4 * share
    SMEM, VMEM = pltpu.SMEM, pltpu.VMEM
    product_flops = 2 * slots * T * T * H

    with jax.named_scope("gather_features"):
        gathered = spread(features, "zh").reshape(N, T, H)
        near = [shift(features, "y", d) for d in range(1, N)]
        near, far = call(
            far_copies_kernel,
            [shape(N, T, H), shape(N, FAR, T, H)],
            [SMEM] + [VMEM] * N,
            name="far_copies",
        )(zh, gathered, *near)
        near_other = swap_cores(near)
        far = exchange(far, "y")
        near_other, far = lax.optimization_barrier((near_other, far))
        far_other = swap_cores(far)
    part = call(
        forward_kernel,
        [shape(row_tiles, T, H)],
        [SMEM] * 4 + [pltpu.HBM] + [VMEM] * 4,
        flops=product_flops,
        scratch=[
            VMEM((slots, T, T), BF16),
            VMEM((col_tiles, T, H), BF16),
            VMEM((row_tiles, T, H), F32),
            pltpu.SemaphoreType.DMA((slots // GROUP,)),
        ],
        name="forward_products",
        limit=VMEM_MOST,
    )(coord_set, core, y, zh, tile_set, near, far, near_other, far_other)
    with jax.named_scope("sum_over_col"):
        part = exchange(part.reshape(NX, NZL, T, H), "x")
        part = call(x_sum_kernel, [shape(NZL, T, H)], [VMEM], name="x_sum")(part)
        part = exchange(part, "zl")
    grads = call(
        dense_kernel,
        [shape(NZL, H + NX * share, T)],
        [VMEM] * 3,
        flops=2 * T * H * H,
        name="dense",
    )(part, weight, grad_out)
    with jax.named_scope("gather_gradients"):
        grads = exchange(grads, "zl")
        common = jnp.broadcast_to(grads[None, :, :H], (NX, NZL, H, T))
        slices = grads[:, H:].reshape(NZL, NX, share, T).transpose(1, 0, 2, 3)
        grads = exchange(jnp.concatenate([common, slices], axis=2), "x")
        grads = grads.reshape(row_tiles, H + share, T)
    rows = FAR * H
    outs = [shape(N, H, T), shape(N * rows + pair_rows, T)]
    mine_near, mine_far, other_near, other_far = call(
        backward_kernel,
        outs + outs,
        [SMEM] * 4 + [VMEM] * 3,
        flops=product_flops,
        scratch=[VMEM((row_tiles, H, T), BF16), VMEM((col_tiles, H, T), F32)],
        name="backward_products",
    )(coord_set, core, y, zh, tile_set, grads, weight)
    with jax.named_scope("sum_over_row"):
        other_far = swap_cores(other_far)
        far = call(core_sum_kernel, [shape(N, rows + pair_rows, T)], [VMEM] * 2, name="core_sum")(mine_far, other_far)
        far = exchange(far, "y")
        other_near = swap_cores(other_near)
        near = call(near_sum_kernel, [shape(H, T)] * N, [VMEM] * 2, name="near_sum")(mine_near, other_near)
        far = call(y_sum_kernel, [shape(N, H + 2 * share, T)], [SMEM, VMEM], name="y_sum")(zh, far)
        far = exchange(far, "zh")
        near = [near[0]] + [shift(near[d], "y", d) for d in range(1, N)]
        grad_features, weight_grad = call(
            last_sum_kernel,
            [shape(T, H), shape(row_tiles, share, H)],
            [VMEM] * 5,
            name="last_sum",
        )(far, *near)
    with jax.named_scope("gather_weight_grad"):
        weight_grad = exchange(weight_grad, COL).reshape(H, H).astype(F32)
    return grad_features, weight_grad


def solution(mesh):
    fine = Mesh(mesh.devices.reshape(tuple(SIZES.values())), tuple(SIZES))
    in_specs = (
        P(COL + ROW, None),
        P(ROW + COL, None),
        P(),
        P(ROW, COL, None, None, None),
        P(ROW, COL, None, None),
    )
    out_specs = (P(COL + ROW, None), P())
    return jax.shard_map(
        on_device, mesh=fine, in_specs=in_specs, out_specs=out_specs, check_vma=False
    )
```
